32 devices in a mesh: groups: 2 (over x), col: 16 (over z, y, core).
Axes of the slice: x: 2, y: 2, z: 4, core: 2. Of those that a mesh axis runs over, the one named last changes fastest.
Arguments:
- field: bfloat16 [3072, 8, 16384], P(('groups', 'col')), parts along dimension 0, may hold values from -6 to 6
- left_first: bfloat16 [16384, 128], replicated, may hold values from -0.046875 to 0.046875
- left_second: bfloat16 [128, 8, 128], replicated, may hold values from -0.1875 to 0.1875
- right_second: bfloat16 [160, 8, 160], replicated, may hold values from -0.15625 to 0.15625
- right_last: bfloat16 [160, 1536], P(None, 'col'), may hold values from -0.15625 to 0.15625
Outputs:
- core_first: float32 [32768, 128], P(('groups', 'col')), parts along dimension 0
- core_middle: float32 [256, 8, 128], P('groups'), parts along dimension 0
- core_last: float32 [3072, 128], P(('groups', 'col')), parts along dimension 0
The draws below stay inside these ranges and needn't reach their ends.
There are 2 independent parts, one for each index of `groups`. The reference program is written for one: setup_inputs(seed, part) draws one part's arguments, and reference() takes and returns one part's arrays. A program takes and returns all parts, laid end to end along the dimension named above; an argument that names none is the same for every part. Nothing has to cross between parts.
All inputs are finite; a program needn't handle non-finite values.
Results may differ from the reference program's by a relative error of at most 0.0098.
Values may be sent and summed in bfloat16 or wider, within the bound.
A program may use at most 128 MiB of HBM per device.

```python
import jax
import jax.numpy as jnp
from jax import lax

COLUMNS = 1536
STEPS = 8
CELLS = 16384
LEFT_RANK = 128
RIGHT_RANK = 160


def with_spikes(result, rng, source, target, parts, factor):
    owner, partner = [(jnp.arange(result.shape[dim]) // (result.shape[dim] // parts)).reshape([-1 if axis == dim else 1 for axis in range(result.ndim)]) for dim in (source, target)]
    chosen = jax.random.permutation(rng, parts)[partner]
    strong = (owner == chosen) | (owner == (partner + parts // 2) % parts)
    return jnp.where(strong, factor * result, result)


def block_scale(own_key, shape, shards, smallest, largest):
    factor_of, own = 1.0, jax.random.fold_in(own_key, 6)
    for axis_at, parts in shards:
        heights = jnp.exp(jax.random.uniform(jax.random.fold_in(own, axis_at), (parts,), jnp.float32, smallest / len(shards), largest / len(shards)))
        factor_of = factor_of * jnp.repeat(heights, shape[axis_at] // parts).reshape([-1 if axis == axis_at else 1 for axis in range(len(shape))])
    return factor_of


def bell_draw(key, shape, deviation, bound, split=(), held_as=jnp.bfloat16):
    result = jax.random.normal(key, shape, jnp.float32) * deviation
    if len(split) > 0:
        result = block_scale(key, shape, split, -0.22, 0.18) * result
    return jnp.clip(result, min=-bound, max=bound).astype(held_as)


def noise_with(stream_key, dims, scale, reach, cuts, heavy, kind=jnp.bfloat16):
    drawn = scale * jax.random.normal(stream_key, dims, jnp.float32)
    if cuts:
        drawn = drawn * block_scale(stream_key, dims, cuts, -0.22, 0.18)
    return jnp.clip(with_spikes(drawn, jax.random.fold_in(stream_key, 3), *heavy), -reach, reach).astype(kind)


def setup_inputs(seed: int = 0, part: int = 0) -> dict:
    splits = jax.random.split(jax.random.key(seed), 6)
    own_keys = jax.random.split(jax.random.fold_in(splits[5], part), 6)
    field = noise_with(own_keys[0], (COLUMNS, STEPS, CELLS), 1.0, 6.0, ((0, 16),), (0, 2, 16, 2.0))
    left_first = bell_draw(splits[1], (CELLS, LEFT_RANK), CELLS ** -0.5, 0.046875)
    left_second = bell_draw(splits[2], (LEFT_RANK, STEPS, LEFT_RANK), (LEFT_RANK * STEPS) ** -0.5, 0.1875)
    right_second = bell_draw(splits[3], (RIGHT_RANK, STEPS, RIGHT_RANK), (RIGHT_RANK * STEPS) ** -0.5, 0.15625)
    right_last = bell_draw(splits[4], (RIGHT_RANK, COLUMNS), COLUMNS ** -0.5, 0.15625, ((1, 16),))
    return dict(field=field, left_first=left_first, left_second=left_second, right_second=right_second, right_last=right_last)


def solve_right(omega):
    gram = jnp.dot(omega, omega.T, precision=lax.Precision.HIGHEST)
    ridge = 0.001 * jnp.trace(gram) / gram.shape[0]
    gram = gram + ridge * jnp.eye(gram.shape[0], dtype=jnp.float32)
    lower = jnp.linalg.cholesky(gram)
    half = lax.linalg.triangular_solve(lower, omega, left_side=True, lower=True)
    return lax.linalg.triangular_solve(lower, half, left_side=True, lower=True, transpose_a=True)

def reference(field, left_first, left_second, right_second, right_last):
    high = lax.Precision.HIGHEST
    cross = jnp.einsum('atb,bc->cta', right_second.astype(jnp.float32), right_last.astype(jnp.float32)).astype(jnp.bfloat16)
    flat = field.reshape(COLUMNS * STEPS, CELLS)
    psi_first = lax.dot_general(flat.astype(jnp.float32), cross.reshape(COLUMNS * STEPS, RIGHT_RANK).astype(jnp.float32), (((0,), (0,)), ((), ())), preferred_element_type=jnp.float32)
    left = jnp.dot(flat.astype(jnp.float32), left_first.astype(jnp.float32), preferred_element_type=jnp.float32).reshape(COLUMNS, STEPS, LEFT_RANK)
    psi_middle = jnp.einsum('ctr,sc->rts', left, right_last.astype(jnp.float32), precision=high)
    core_last = jnp.einsum('ctr,rtq->cq', left, left_second.astype(jnp.float32), precision=high)
    omega_first = jnp.dot(left_first.astype(jnp.float32).T, psi_first, precision=high)
    omega_middle = jnp.einsum('rtq,rts->qs', left_second.astype(jnp.float32), psi_middle, precision=high)
    core_first = jnp.dot(psi_first, solve_right(omega_first).T, precision=high)
    core_middle = jnp.einsum('rts,qs->rtq', psi_middle, solve_right(omega_middle), precision=high)
    return (core_first, core_middle, core_last)
```

```python
import functools

import jax
import jax.numpy as jnp
from jax import lax
from jax.experimental import pallas as pl
from jax.experimental.pallas import tpu as pltpu
from jax.sharding import PartitionSpec as P

HIGH = lax.Precision.HIGHEST
MESH = pl.DeviceIdType.MESH


def solve_right(omega):
    gram = jnp.dot(omega, omega.T, precision=HIGH)
    ridge = 0.001 * jnp.trace(gram) / gram.shape[0]
    gram = gram + ridge * jnp.eye(gram.shape[0], dtype=jnp.float32)
    lower = jnp.linalg.cholesky(gram)
    half = lax.linalg.triangular_solve(lower, omega, left_side=True, lower=True)
    return lax.linalg.triangular_solve(lower, half, left_side=True, lower=True, transpose_a=True)


def remote(src, dst, send_sem, recv_sem, target):
    return pltpu.make_async_remote_copy(
        src_ref=src, dst_ref=dst, send_sem=send_sem, recv_sem=recv_sem,
        device_id={"col": target}, device_id_type=MESH,
    )


def sketch_kernel(
    n, cross_ref, field_ref, wide_ref, half_ref, psi_ref, wide_out, half_out,
    chunk, a_send, a_recv, a_keep, b_send, b_recv, b_keep, c_send, c_recv,
    w_recv, h_recv, w_all, h_all,
    load_sem, a_ss, a_rs, b_ss, b_rs, c_ss, c_rs, w_ss, w_rs, h_ss, h_rs, w2_ss, w2_rs, h2_ss, h2_rs,
):
    far = n // 4
    me = lax.axis_index("col")
    core = lax.rem(me, 2)
    y = lax.rem(me // 2, 2)
    z = me // 4
    block = psi_ref.shape[1]
    span = 4 * block

    def goal(k):
        return lax.rem(z + 1 + k, far)

    def load(k):
        start = pl.multiple_of(goal(k) * span, span)
        return pltpu.make_async_copy(field_ref.at[:, pl.ds(start, span)], chunk.at[k % 2], load_sem.at[k % 2])

    load(0).start()
    barrier = pltpu.get_barrier_semaphore()

    @pl.loop(1, n)
    def _(j):
        pl.semaphore_signal(barrier, inc=1, device_id={"col": lax.rem(me + j, n)}, device_id_type=MESH)

    pl.semaphore_wait(barrier, n - 1)

    def spread_wide(j):
        to = lax.rem(me + j, n)
        return remote(wide_ref.at[to], w_recv.at[j], w_ss.at[j], w_rs.at[j], to)

    def spread_half(j):
        to = lax.rem(me + j, n)
        return remote(half_ref.at[to], h_recv.at[j], h_ss.at[j], h_rs.at[j], to)

    def share_wide(j):
        return remote(w_all.at[0], w_all.at[j], w2_ss.at[j], w2_rs.at[j], lax.rem(me + j, n))

    def share_half(j):
        return remote(h_all.at[0], h_all.at[j], h2_ss.at[j], h2_rs.at[j], lax.rem(me + j, n))

    @pl.loop(1, n)
    def _(j):
        spread_wide(j).start()
        spread_half(j).start()

    def copy_a(k):
        return remote(a_send.at[k], a_recv.at[k], a_ss.at[k], a_rs.at[k], me + 1 - 2 * core)

    def copy_b(k):
        return remote(b_send.at[k], b_recv.at[k], b_ss.at[k], b_rs.at[k], me + 2 - 4 * y)

    def copy_c(k):
        return remote(c_send.at[k], c_recv.at[k], c_ss.at[k], c_rs.at[k], (goal(k) * 2 + y) * 2 + core)

    def product(k, row, which):
        start = pl.multiple_of((row * 2 + which) * block, block)
        return jnp.dot(cross_ref[...], chunk[k % 2, :, pl.ds(start, block)], preferred_element_type=jnp.float32)

    def compute(k):
        if k + 1 < far:
            load(k + 1).start()
        load(k).wait()
        for row in range(2):
            a_send[k, row] = product(k, row, 1 - core).astype(jnp.bfloat16)
        copy_a(k).start()
        for row in range(2):
            a_keep[k, row] = product(k, row, core)

    def stage_b(k):
        copy_a(k).wait()
        b_send[k] = (a_keep[k, 1 - y] + a_recv[k, 1 - y].astype(jnp.float32)).astype(jnp.bfloat16)
        copy_b(k).start()
        b_keep[k] = a_keep[k, y] + a_recv[k, y].astype(jnp.float32)

    def stage_c(k):
        copy_b(k).wait()
        total = b_keep[k] + b_recv[k].astype(jnp.float32)
        if k < far - 1:
            c_send[k] = total.astype(jnp.bfloat16)
            copy_c(k).start()
        else:
            psi_ref[...] = total

    for k in range(far + 2):
        if k < far:
            compute(k)
        if 1 <= k <= far:
            stage_b(k - 1)
        if k == min(1, far - 1):

            @pl.loop(1, n)
            def _(j):
                spread_wide(j).wait()
                spread_half(j).wait()

            w_all[0] = lax.fori_loop(1, n, lambda j, s: s + w_recv[j], wide_ref[me])
            h_all[0] = lax.fori_loop(
                1, n, lambda j, s: s + h_recv[j].astype(jnp.float32), half_ref[me].astype(jnp.float32)
            ).astype(jnp.bfloat16)

            @pl.loop(1, n)
            def _(j):
                share_wide(j).start()
                share_half(j).start()

        if k >= 2:
            stage_c(k - 2)

    @pl.loop(1, n)
    def _(j):
        share_wide(j).wait()
        share_half(j).wait()

    wide_out[me] = w_all[0]
    half_out[me] = h_all[0]

    @pl.loop(1, n)
    def _(j):
        source = lax.rem(me - j + n, n)
        wide_out[source] = w_all[j]
        half_out[source] = h_all[j]

    for k in range(far - 1):
        copy_c(k).wait()
        psi_ref[...] += c_recv[k].astype(jnp.float32)


def sketch(n, cross, flat, wide, half):
    rank, depth = cross.shape
    cells = flat.shape[1]
    block, far = cells // n, n // 4
    low, full = jnp.bfloat16, jnp.float32
    dma = pltpu.SemaphoreType.DMA
    vmem = pl.BlockSpec(memory_space=pltpu.VMEM)
    return pl.pallas_call(
        functools.partial(sketch_kernel, n),
        out_shape=(
            jax.ShapeDtypeStruct((rank, block), full),
            jax.ShapeDtypeStruct(wide.shape, full),
            jax.ShapeDtypeStruct(half.shape, low),
        ),
        in_specs=[vmem, pl.BlockSpec(memory_space=pl.ANY), vmem, vmem],
        out_specs=(vmem, vmem, vmem),
        scratch_shapes=[
            pltpu.VMEM((2, depth, 4 * block), low),
            pltpu.VMEM((far, 2, rank, block), low),
            pltpu.VMEM((far, 2, rank, block), low),
            pltpu.VMEM((far, 2, rank, block), full),
            pltpu.VMEM((far, rank, block), low),
            pltpu.VMEM((far, rank, block), low),
            pltpu.VMEM((far, rank, block), full),
            pltpu.VMEM((far, rank, block), low),
            pltpu.VMEM((far, rank, block), low),
            pltpu.VMEM(wide.shape, full),
            pltpu.VMEM(half.shape, low),
            pltpu.VMEM(wide.shape, full),
            pltpu.VMEM(half.shape, low),
            dma((2,)),
            *[dma((far,)) for _ in range(6)],
            *[dma((n,)) for _ in range(8)],
        ],
        compiler_params=pltpu.CompilerParams(
            collective_id=0, has_side_effects=True, vmem_limit_bytes=56 * 2**20
        ),
        cost_estimate=pl.CostEstimate(
            flops=2 * rank * depth * cells, bytes_accessed=2 * depth * cells, transcendentals=0
        ),
    )(cross, flat, wide, half)


def split_rows(x, n, tile):
    rows = -(-x.size // (n * 128))
    rows = -(-rows // tile) * tile
    x = jnp.pad(x.reshape(-1), (0, n * rows * 128 - x.size))
    return x.reshape(n, rows, 128)


def body(n, field, left_first, left_second, right_second, right_last):
    col_count, steps, cells = field.shape
    rank_left = left_first.shape[1]
    rank_right = right_second.shape[0]
    flat = field.reshape(col_count * steps, cells)
    cross = jnp.einsum(
        "atb,bc->act", right_second, right_last, preferred_element_type=jnp.float32
    ).astype(jnp.bfloat16).reshape(rank_right, col_count * steps)
    left = jnp.dot(flat, left_first, preferred_element_type=jnp.float32)
    left_wide = left.reshape(col_count, steps, rank_left)
    last_wide = right_last.astype(jnp.float32)
    middle_term = jnp.einsum("ctr,sc->rts", left_wide, last_wide, precision=HIGH)
    core_last = jnp.einsum("ctr,rtq->cq", left_wide, left_second.astype(jnp.float32), precision=HIGH)
    omega_first_term = jnp.einsum("kr,ak->ra", left, cross.astype(jnp.float32), precision=HIGH)
    omega_middle_term = jnp.einsum("cq,ac->qa", core_last, last_wide, precision=HIGH)
    omega_term = jnp.stack([omega_first_term, omega_middle_term])
    psi, wide, half = sketch(
        n, cross, flat, split_rows(omega_term, n, 8), split_rows(middle_term.astype(jnp.bfloat16), n, 16)
    )
    omega = wide.reshape(-1)[: omega_term.size].reshape(omega_term.shape)
    psi_middle = half.reshape(-1)[: middle_term.size].reshape(middle_term.shape).astype(jnp.float32)
    core_first = jnp.einsum("ag,ra->gr", psi, solve_right(omega[0]), precision=HIGH)
    core_middle = jnp.einsum("rts,qs->rtq", psi_middle, solve_right(omega[1]), precision=HIGH)
    return (core_first, core_middle, core_last)


def solution(mesh):
    return jax.shard_map(
        functools.partial(body, mesh.shape["col"]),
        mesh=mesh,
        in_specs=(P(("groups", "col"), None, None), P(), P(), P(), P(None, "col")),
        out_specs=(P(("groups", "col"), None), P("groups", None, None), P(("groups", "col"), None)),
        check_vma=False,
    )
```

```python
import functools

import jax
import jax.numpy as jnp
from jax import lax
from jax.experimental import pallas as pl
from jax.experimental.pallas import tpu as pltpu
from jax.sharding import PartitionSpec as P

HIGH = lax.Precision.HIGHEST
MESH = pl.DeviceIdType.MESH


def ridged_gram(omega):
    gram = lax.dot_general(
        omega, omega, (((1,), (1,)), ((), ())), precision=HIGH, preferred_element_type=jnp.float32
    )
    rank = gram.shape[0]
    eye = lax.broadcasted_iota(jnp.int32, gram.shape, 0) == lax.broadcasted_iota(jnp.int32, gram.shape, 1)
    trace = jnp.sum(jnp.where(eye, gram, 0.0))
    return gram + jnp.where(eye, 0.001 * trace / rank, 0.0)


def eliminate(gram, k):
    rank = gram.shape[0]
    at_k = lax.broadcasted_iota(jnp.int32, (1, rank), 1) == k
    column = jnp.broadcast_to(gram[:, k : k + 1], gram.shape)
    row = jnp.where(at_k, 1.0, gram[k : k + 1, :]) / column[k : k + 1, :]
    result = jnp.where(at_k, 0.0, gram) - column * row
    rows = lax.broadcasted_iota(jnp.int32, (8, rank), 0)
    head = jnp.where(rows == k, row, result[:8])
    return jnp.concatenate([head, result[8:]], axis=0)


def solve_pair(first, second):
    rank = first.shape[0]

    def eight(_, pair):
        for k in range(8):
            pair = tuple(eliminate(gram, k) for gram in pair)
        pair = tuple(jnp.concatenate([gram[8:], gram[:8]], axis=0) for gram in pair)
        return tuple(pltpu.roll(gram, rank - 8, 1) for gram in pair)

    pair = lax.fori_loop(0, rank // 8, eight, (ridged_gram(first), ridged_gram(second)))
    return [
        jnp.dot(inverse, omega, precision=HIGH, preferred_element_type=jnp.float32)
        for inverse, omega in zip(pair, (first, second))
    ]


def remote(src, dst, send_sem, recv_sem, target):
    return pltpu.make_async_remote_copy(
        src_ref=src, dst_ref=dst, send_sem=send_sem, recv_sem=recv_sem,
        device_id={"col": target}, device_id_type=MESH,
    )


def sketch_kernel(
    n, rows, cross_ref, field_ref, wide_ref, half_ref, psi_ref, factor_out, half_out,
    chunk, a_send, a_recv, a_keep, b_send, b_recv, b_keep, c_send, c_recv,
    w_recv, h_recv, w_all, h_all, omega_ref,
    load_sem, a_ss, a_rs, b_ss, b_rs, c_ss, c_rs, w_ss, w_rs, h_ss, h_rs, w2_ss, w2_rs, h2_ss, h2_rs,
):
    far = n // 4
    me = lax.axis_index("col")
    core = lax.rem(me, 2)
    y = lax.rem(me // 2, 2)
    z = me // 4
    block = psi_ref.shape[1]
    span = 4 * block

    def goal(k):
        return lax.rem(z + 1 + k, far)

    def load(k):
        start = pl.multiple_of(goal(k) * span, span)
        return pltpu.make_async_copy(field_ref.at[:, pl.ds(start, span)], chunk.at[k % 2], load_sem.at[k % 2])

    load(0).start()
    barrier = pltpu.get_barrier_semaphore()

    @pl.loop(1, n)
    def _(j):
        pl.semaphore_signal(barrier, inc=1, device_id={"col": lax.rem(me + j, n)}, device_id_type=MESH)

    pl.semaphore_wait(barrier, n - 1)

    def spread_wide(j):
        to = lax.rem(me + j, n)
        return remote(wide_ref.at[to], w_recv.at[j], w_ss.at[j], w_rs.at[j], to)

    def spread_half(j):
        to = lax.rem(me + j, n)
        return remote(half_ref.at[to], h_recv.at[j], h_ss.at[j], h_rs.at[j], to)

    def share_wide(j):
        return remote(w_all.at[0], w_all.at[j], w2_ss.at[j], w2_rs.at[j], lax.rem(me + j, n))

    def share_half(j):
        return remote(h_all.at[0], h_all.at[j], h2_ss.at[j], h2_rs.at[j], lax.rem(me + j, n))

    @pl.loop(1, n)
    def _(j):
        spread_wide(j).start()
        spread_half(j).start()

    def copy_a(k):
        return remote(a_send.at[k], a_recv.at[k], a_ss.at[k], a_rs.at[k], me + 1 - 2 * core)

    def copy_b(k):
        return remote(b_send.at[k], b_recv.at[k], b_ss.at[k], b_rs.at[k], me + 2 - 4 * y)

    def copy_c(k):
        return remote(c_send.at[k], c_recv.at[k], c_ss.at[k], c_rs.at[k], (goal(k) * 2 + y) * 2 + core)

    def product(k, row, which):
        start = pl.multiple_of((row * 2 + which) * block, block)
        return jnp.dot(cross_ref[...], chunk[k % 2, :, pl.ds(start, block)], preferred_element_type=jnp.float32)

    def compute(k):
        if k + 1 < far:
            load(k + 1).start()
        load(k).wait()
        for row in range(2):
            a_send[k, row] = product(k, row, 1 - core).astype(jnp.bfloat16)
        copy_a(k).start()
        for row in range(2):
            a_keep[k, row] = product(k, row, core)

    def stage_b(k):
        copy_a(k).wait()
        b_send[k] = (a_keep[k, 1 - y] + a_recv[k, 1 - y].astype(jnp.float32)).astype(jnp.bfloat16)
        copy_b(k).start()
        b_keep[k] = a_keep[k, y] + a_recv[k, y].astype(jnp.float32)

    def stage_c(k):
        copy_b(k).wait()
        total = b_keep[k] + b_recv[k].astype(jnp.float32)
        if k < far - 1:
            c_send[k] = total.astype(jnp.bfloat16)
            copy_c(k).start()
        else:
            psi_ref[...] = total

    def solve():
        @pl.loop(1, n)
        def _(j):
            share_wide(j).wait()
            share_half(j).wait()

        omega_ref[me] = w_all[0]
        half_out[me] = h_all[0]

        @pl.loop(1, n)
        def _(j):
            source = lax.rem(me - j + n, n)
            omega_ref[source] = w_all[j]
            half_out[source] = h_all[j]

        held = omega_ref.shape[1]
        omega = omega_ref[...].reshape(n * held, omega_ref.shape[2])
        if held != rows:
            to = lax.broadcasted_iota(jnp.int32, (n * rows, n * held), 0)
            at = lax.broadcasted_iota(jnp.int32, (n * rows, n * held), 1)
            chosen = (to == (at // held) * rows + at % held) & (at % held < rows)
            omega = jnp.dot(chosen.astype(jnp.float32), omega, precision=HIGH, preferred_element_type=jnp.float32)
        rank = n * rows // 2
        factor_out[0], factor_out[1] = solve_pair(omega[:rank], omega[rank:])

    for k in range(far + 2):
        if k < far:
            compute(k)
        if 1 <= k <= far:
            stage_b(k - 1)
        if k == min(1, far - 1):

            @pl.loop(1, n)
            def _(j):
                spread_wide(j).wait()
                spread_half(j).wait()

            w_all[0] = lax.fori_loop(1, n, lambda j, s: s + w_recv[j], wide_ref[me])
            h_all[0] = lax.fori_loop(
                1, n, lambda j, s: s + h_recv[j].astype(jnp.float32), half_ref[me].astype(jnp.float32)
            ).astype(jnp.bfloat16)

            @pl.loop(1, n)
            def _(j):
                share_wide(j).start()
                share_half(j).start()

        if k == far + 1:
            solve()
        if k >= 2:
            stage_c(k - 2)

    for k in range(far - 1):
        copy_c(k).wait()
        psi_ref[...] += c_recv[k].astype(jnp.float32)


def sketch(n, rows, cross, flat, wide, half):
    rank, depth = cross.shape
    cells = flat.shape[1]
    block, far = cells // n, n // 4
    low, full = jnp.bfloat16, jnp.float32
    dma = pltpu.SemaphoreType.DMA
    vmem = pl.BlockSpec(memory_space=pltpu.VMEM)
    return pl.pallas_call(
        functools.partial(sketch_kernel, n, rows),
        out_shape=(
            jax.ShapeDtypeStruct((rank, block), full),
            jax.ShapeDtypeStruct((2, n * rows // 2, rank), full),
            jax.ShapeDtypeStruct(half.shape, low),
        ),
        in_specs=[vmem, pl.BlockSpec(memory_space=pl.ANY), vmem, vmem],
        out_specs=(vmem, vmem, vmem),
        scratch_shapes=[
            pltpu.VMEM((2, depth, 4 * block), low),
            pltpu.VMEM((far, 2, rank, block), low),
            pltpu.VMEM((far, 2, rank, block), low),
            pltpu.VMEM((far, 2, rank, block), full),
            pltpu.VMEM((far, rank, block), low),
            pltpu.VMEM((far, rank, block), low),
            pltpu.VMEM((far, rank, block), full),
            pltpu.VMEM((far, rank, block), low),
            pltpu.VMEM((far, rank, block), low),
            pltpu.VMEM(wide.shape, full),
            pltpu.VMEM(half.shape, low),
            pltpu.VMEM(wide.shape, full),
            pltpu.VMEM(half.shape, low),
            pltpu.VMEM(wide.shape, full),
            dma((2,)),
            *[dma((far,)) for _ in range(6)],
            *[dma((n,)) for _ in range(8)],
        ],
        compiler_params=pltpu.CompilerParams(
            collective_id=0, has_side_effects=True, vmem_limit_bytes=56 * 2**20
        ),
        cost_estimate=pl.CostEstimate(
            flops=2 * rank * depth * cells, bytes_accessed=2 * depth * cells, transcendentals=0
        ),
    )(cross, flat, wide, half)


def split_rows(x, n, tile):
    rows = -(-x.size // (n * 128))
    rows = -(-rows // tile) * tile
    x = jnp.pad(x.reshape(-1), (0, n * rows * 128 - x.size))
    return x.reshape(n, rows, 128)


def body(n, field, left_first, left_second, right_second, right_last):
    col_count, steps, cells = field.shape
    rank_left = left_first.shape[1]
    rank_right = right_second.shape[0]
    flat = field.reshape(col_count * steps, cells)
    cross = jnp.einsum(
        "atb,bc->act", right_second, right_last, preferred_element_type=jnp.float32
    ).astype(jnp.bfloat16).reshape(rank_right, col_count * steps)
    left = jnp.dot(flat, left_first, preferred_element_type=jnp.float32)
    left_wide = left.reshape(col_count, steps, rank_left)
    last_wide = right_last.astype(jnp.float32)
    middle_term = jnp.einsum("ctr,sc->rts", left_wide, last_wide, precision=HIGH)
    core_last = jnp.einsum("ctr,rtq->cq", left_wide, left_second.astype(jnp.float32), precision=HIGH)
    omega_first_term = jnp.einsum("kr,ak->ra", left, cross.astype(jnp.float32), precision=HIGH)
    omega_middle_term = jnp.einsum("cq,ac->qa", core_last, last_wide, precision=HIGH)
    omega_term = jnp.stack([omega_first_term, omega_middle_term])
    rows = 2 * rank_left // n
    held = -(-rows // 8) * 8
    omega_term = jnp.pad(omega_term.reshape(n, rows, rank_right), ((0, 0), (0, held - rows), (0, 0)))
    psi, factor, half = sketch(
        n, rows, cross, flat, omega_term, split_rows(middle_term.astype(jnp.bfloat16), n, 16)
    )
    psi_middle = half.reshape(-1)[: middle_term.size].reshape(middle_term.shape).astype(jnp.float32)
    core_first = jnp.einsum("ag,ra->gr", psi, factor[0], precision=HIGH)
    core_middle = jnp.einsum("rts,qs->rtq", psi_middle, factor[1], precision=HIGH)
    return (core_first, core_middle, core_last)


def solution(mesh):
    return jax.shard_map(
        functools.partial(body, mesh.shape["col"]),
        mesh=mesh,
        in_specs=(P(("groups", "col"), None, None), P(), P(), P(), P(None, "col")),
        out_specs=(P(("groups", "col"), None), P("groups", None, None), P(("groups", "col"), None)),
        check_vma=False,
    )
```

```python
import functools

import jax
import jax.numpy as jnp
from jax import lax
from jax.experimental import pallas as pl
from jax.experimental.pallas import tpu as pltpu
from jax.sharding import PartitionSpec as P

HIGH = lax.Precision.HIGHEST
MESH = pl.DeviceIdType.MESH


def ridged_gram(omega):
    gram = lax.dot_general(
        omega, omega, (((1,), (1,)), ((), ())), precision=HIGH, preferred_element_type=jnp.float32
    )
    rank = gram.shape[0]
    eye = lax.broadcasted_iota(jnp.int32, gram.shape, 0) == lax.broadcasted_iota(jnp.int32, gram.shape, 1)
    trace = jnp.sum(jnp.where(eye, gram, 0.0))
    return gram + jnp.where(eye, 0.001 * trace / rank, 0.0)


def eliminate(gram, k):
    rank = gram.shape[0]
    at_k = lax.broadcasted_iota(jnp.int32, (1, rank), 1) == k
    column = jnp.broadcast_to(gram[:, k : k + 1], gram.shape)
    row = jnp.where(at_k, 1.0, gram[k : k + 1, :]) / column[k : k + 1, :]
    result = jnp.where(at_k, 0.0, gram) - column * row
    rows = lax.broadcasted_iota(jnp.int32, (8, rank), 0)
    head = jnp.where(rows == k, row, result[:8])
    return jnp.concatenate([head, result[8:]], axis=0)


def solve_pair(first, second):
    rank = first.shape[0]

    def eight(_, pair):
        for k in range(8):
            pair = tuple(eliminate(gram, k) for gram in pair)
        pair = tuple(jnp.concatenate([gram[8:], gram[:8]], axis=0) for gram in pair)
        return tuple(pltpu.roll(gram, rank - 8, 1) for gram in pair)

    pair = lax.fori_loop(0, rank // 8, eight, (ridged_gram(first), ridged_gram(second)))
    return [
        jnp.dot(inverse, omega, precision=HIGH, preferred_element_type=jnp.float32)
        for inverse, omega in zip(pair, (first, second))
    ]


def remote(src, dst, send_sem, recv_sem, target):
    return pltpu.make_async_remote_copy(
        src_ref=src, dst_ref=dst, send_sem=send_sem, recv_sem=recv_sem,
        device_id={"col": target}, device_id_type=MESH,
    )


def sketch_kernel(
    n, rows, cross_ref, field_ref, wide_ref, half_ref, psi_ref, factor_out, half_out,
    chunk, a_send, a_recv, a_keep, b_send, b_recv, b_keep, c_send, c_recv,
    w_a, w_ak, w_b, w_bk, w_c, w_all, h_a, h_ak, h_b, h_bk, h_c, h_all,
    load_sem, a_ss, a_rs, b_ss, b_rs, c_ss, c_rs, w_ss, w_rs, h_ss, h_rs,
):
    far = n // 4
    me = lax.axis_index("col")
    core = lax.rem(me, 2)
    y = lax.rem(me // 2, 2)
    z = me // 4
    block = psi_ref.shape[1]
    span = 4 * block

    def goal(k):
        return lax.rem(z + 1 + k, far)

    def load(k):
        start = pl.multiple_of(goal(k) * span, span)
        return pltpu.make_async_copy(field_ref.at[:, pl.ds(start, span)], chunk.at[k % 2], load_sem.at[k % 2])

    load(0).start()
    barrier = pltpu.get_barrier_semaphore()

    @pl.loop(1, n)
    def _(j):
        pl.semaphore_signal(barrier, inc=1, device_id={"col": lax.rem(me + j, n)}, device_id_type=MESH)

    pl.semaphore_wait(barrier, n - 1)

    small = (
        (wide_ref, w_a, w_ak, w_b, w_bk, w_c, w_all, w_ss, w_rs),
        (half_ref, h_a, h_ak, h_b, h_bk, h_c, h_all, h_ss, h_rs),
    )
    other_core, other_y = me + 1 - 2 * core, me + 2 - 4 * y

    def small_copies(stage):
        found = []
        for source, a, ak, b, bk, c, whole, ss, rs in small:
            mine = whole.at[z, y, core]
            if stage == 0:
                parts = [(source.at[:, :, 1 - core], a, 0, other_core)]
            elif stage == 1:
                parts = [(ak.at[:, 1 - y], b, 1, other_y)]
            elif stage == 2:
                parts = [(bk.at[goal(k)], c.at[k], 4 + k, (goal(k) * 2 + y) * 2 + core) for k in range(far - 1)]
            elif stage == 3:
                parts = [(mine, mine, 3 + far + k, (goal(k) * 2 + y) * 2 + core) for k in range(far - 1)]
            elif stage == 4:
                parts = [(whole.at[:, y, core], whole.at[:, y, core], 2, other_y)]
            else:
                parts = [(whole.at[:, :, core], whole.at[:, :, core], 3, other_core)]
            found += [remote(src, dst, ss.at[i], rs.at[i], to) for src, dst, i, to in parts]
        return found

    def small_start(stage):
        for copy in small_copies(stage):
            copy.start()

    def small_finish(stage):
        for copy in small_copies(stage):
            copy.wait()
        for source, a, ak, b, bk, c, whole, _, _ in small:
            if stage == 0:
                ak[...] = (source[:, :, core].astype(jnp.float32) + a[...].astype(jnp.float32)).astype(ak.dtype)
            elif stage == 1:
                bk[...] = (ak[:, y].astype(jnp.float32) + b[...].astype(jnp.float32)).astype(bk.dtype)
            elif stage == 2:
                total = bk[z].astype(jnp.float32)
                for k in range(far - 1):
                    total += c[k].astype(jnp.float32)
                whole[z, y, core] = total.astype(whole.dtype)

    small_start(0)

    def copy_a(k):
        return remote(a_send.at[k], a_recv.at[k], a_ss.at[k], a_rs.at[k], me + 1 - 2 * core)

    def copy_b(k):
        return remote(b_send.at[k], b_recv.at[k], b_ss.at[k], b_rs.at[k], me + 2 - 4 * y)

    def copy_c(k):
        return remote(c_send.at[k], c_recv.at[k], c_ss.at[k], c_rs.at[k], (goal(k) * 2 + y) * 2 + core)

    def product(k, row, which):
        start = pl.multiple_of((row * 2 + which) * block, block)
        return jnp.dot(cross_ref[...], chunk[k % 2, :, pl.ds(start, block)], preferred_element_type=jnp.float32)

    def compute(k):
        if k + 1 < far:
            load(k + 1).start()
        load(k).wait()
        for row in range(2):
            a_send[k, row] = product(k, row, 1 - core).astype(jnp.bfloat16)
        copy_a(k).start()
        for row in range(2):
            a_keep[k, row] = product(k, row, core)

    def stage_b(k):
        copy_a(k).wait()
        b_send[k] = (a_keep[k, 1 - y] + a_recv[k, 1 - y].astype(jnp.float32)).astype(jnp.bfloat16)
        copy_b(k).start()
        b_keep[k] = a_keep[k, y] + a_recv[k, y].astype(jnp.float32)

    def stage_c(k):
        copy_b(k).wait()
        total = b_keep[k] + b_recv[k].astype(jnp.float32)
        if k < far - 1:
            c_send[k] = total.astype(jnp.bfloat16)
            copy_c(k).start()
        else:
            psi_ref[...] = total

    def solve():
        small_finish(5)
        half_out[...] = h_all[...]
        held = w_all.shape[3]
        omega = w_all[...].reshape(n * held, w_all.shape[4])
        if held != rows:
            to = lax.broadcasted_iota(jnp.int32, (n * rows, n * held), 0)
            at = lax.broadcasted_iota(jnp.int32, (n * rows, n * held), 1)
            chosen = (to == (at // held) * rows + at % held) & (at % held < rows)
            omega = jnp.dot(chosen.astype(jnp.float32), omega, precision=HIGH, preferred_element_type=jnp.float32)
        rank = n * rows // 2
        factor_out[0], factor_out[1] = solve_pair(omega[:rank], omega[rank:])

    for k in range(far + 2):
        if k < far:
            compute(k)
        if 1 <= k <= far:
            stage_b(k - 1)
        stage = k - max(far - 4, 0)
        if 0 <= stage < 5:
            small_finish(stage)
            small_start(stage + 1)
        if k == far + 1:
            solve()
        if k >= 2:
            stage_c(k - 2)

    for k in range(far - 1):
        copy_c(k).wait()
        psi_ref[...] += c_recv[k].astype(jnp.float32)


def sketch(n, rows, cross, flat, wide, half):
    rank, depth = cross.shape
    cells = flat.shape[1]
    block, far = cells // n, n // 4
    low, full = jnp.bfloat16, jnp.float32
    dma = pltpu.SemaphoreType.DMA
    vmem = pl.BlockSpec(memory_space=pltpu.VMEM)
    return pl.pallas_call(
        functools.partial(sketch_kernel, n, rows),
        out_shape=(
            jax.ShapeDtypeStruct((rank, block), full),
            jax.ShapeDtypeStruct((2, n * rows // 2, rank), full),
            jax.ShapeDtypeStruct(half.shape, low),
        ),
        in_specs=[vmem, pl.BlockSpec(memory_space=pl.ANY), vmem, vmem],
        out_specs=(vmem, vmem, vmem),
        scratch_shapes=[
            pltpu.VMEM((2, depth, 4 * block), low),
            pltpu.VMEM((far, 2, rank, block), low),
            pltpu.VMEM((far, 2, rank, block), low),
            pltpu.VMEM((far, 2, rank, block), full),
            pltpu.VMEM((far, rank, block), low),
            pltpu.VMEM((far, rank, block), low),
            pltpu.VMEM((far, rank, block), full),
            pltpu.VMEM((far, rank, block), low),
            pltpu.VMEM((far, rank, block), low),
            *[
                pltpu.VMEM(lead + x.shape[3:], x.dtype)
                for x in (wide, half)
                for lead in ((far, 2), (far, 2), (far,), (far,), (far,), (far, 2, 2))
            ],
            dma((2,)),
            *[dma((far,)) for _ in range(6)],
            *[dma((2 * far + 2,)) for _ in range(4)],
        ],
        compiler_params=pltpu.CompilerParams(
            collective_id=0, has_side_effects=True, vmem_limit_bytes=56 * 2**20
        ),
        cost_estimate=pl.CostEstimate(
            flops=2 * rank * depth * cells, bytes_accessed=2 * depth * cells, transcendentals=0
        ),
    )(cross, flat, wide, half)


def split_rows(x, n, tile):
    rows = -(-x.size // (n * 128))
    rows = -(-rows // tile) * tile
    x = jnp.pad(x.reshape(-1), (0, n * rows * 128 - x.size))
    return x.reshape(n, rows, 128)


def body(n, field, left_first, left_second, right_second, right_last):
    col_count, steps, cells = field.shape
    rank_left = left_first.shape[1]
    rank_right = right_second.shape[0]
    flat = field.reshape(col_count * steps, cells)
    cross = jnp.einsum(
        "atb,bc->act", right_second, right_last, preferred_element_type=jnp.float32
    ).astype(jnp.bfloat16).reshape(rank_right, col_count * steps)
    left = jnp.dot(flat, left_first, preferred_element_type=jnp.float32)
    left_wide = left.reshape(col_count, steps, rank_left)
    last_wide = right_last.astype(jnp.float32)
    middle_term = jnp.einsum("ctr,sc->rts", left_wide, last_wide, precision=HIGH)
    core_last = jnp.einsum("ctr,rtq->cq", left_wide, left_second.astype(jnp.float32), precision=HIGH)
    omega_first_term = jnp.einsum("kr,ak->ra", left, cross.astype(jnp.float32), precision=HIGH)
    omega_middle_term = jnp.einsum("cq,ac->qa", core_last, last_wide, precision=HIGH)
    omega_term = jnp.stack([omega_first_term, omega_middle_term])
    rows = 2 * rank_left // n
    held = -(-rows // 8) * 8
    omega_term = jnp.pad(omega_term.reshape(n, rows, rank_right), ((0, 0), (0, held - rows), (0, 0)))
    middle_rows = split_rows(middle_term.astype(jnp.bfloat16), n, 16)
    psi, factor, half = sketch(
        n, rows, cross, flat,
        omega_term.reshape(n // 4, 2, 2, *omega_term.shape[1:]),
        middle_rows.reshape(n // 4, 2, 2, *middle_rows.shape[1:]),
    )
    psi_middle = half.reshape(-1)[: middle_term.size].reshape(middle_term.shape).astype(jnp.float32)
    core_first = jnp.einsum("ag,ra->gr", psi, factor[0], precision=HIGH)
    core_middle = jnp.einsum("rts,qs->rtq", psi_middle, factor[1], precision=HIGH)
    return (core_first, core_middle, core_last)


def solution(mesh):
    return jax.shard_map(
        functools.partial(body, mesh.shape["col"]),
        mesh=mesh,
        in_specs=(P(("groups", "col"), None, None), P(), P(), P(), P(None, "col")),
        out_specs=(P(("groups", "col"), None), P("groups", None, None), P(("groups", "col"), None)),
        check_vma=False,
    )
```
